32 devices in a mesh: ctx: 8 (over y, x, core), exp: 4 (over z).
Axes of the slice: x: 2, y: 2, z: 4, core: 2. Of those that a mesh axis runs over, the one named last changes fastest.
Arguments:
- queries: bfloat16 [4, 1024, 4096], P('exp', 'ctx'), may hold values from -4.5 to 4.5
- keys: bfloat16 [4, 1024, 256], P('exp', 'ctx'), may hold values from -4.5 to 4.5
- values: bfloat16 [4, 1024, 256], P('exp', 'ctx'), may hold values from -12 to 12
- attention_output_grad: bfloat16 [4, 1024, 4096], P('exp', 'ctx'), may hold values from -18 to 18
- span_order: int32 [4, 16], P('exp'), may hold values from 0 to 15, each once within a row
- out_grad: bfloat16 [4, 1024, 4096], P('exp', 'ctx'), may hold values from -6 to 6
- routes: int32 [4, 1024, 2], P('exp', 'ctx'), may hold values from 0 to 15, all different within a row; in each aligned block of 128 rows (0 to 127, 128 to 255, ..., all dimensions but the last counted through in order) at most 24 rows name the same one
- combine: float32 [4, 1024, 2], P('exp', 'ctx'), may hold values from 0.1 to 1
- w_gate: bfloat16 [32, 4096, 768], P(('ctx', 'exp')), may hold values from -0.09375 to 0.09375
- w_up: bfloat16 [32, 4096, 768], P(('ctx', 'exp')), may hold values from -0.09375 to 0.09375
- w_down: bfloat16 [32, 768, 4096], P(('ctx', 'exp')), may hold values from -0.15625 to 0.15625
- gate_up_saved: bfloat16 [32, 32, 24, 1536], P(('ctx', 'exp')), may hold values from -6 to 6
Outputs:
- query_grad: bfloat16 [4, 1024, 4096], P('exp', 'ctx')
- key_grad: bfloat16 [4, 1024, 256], P('exp', 'ctx')
- value_grad: bfloat16 [4, 1024, 256], P('exp', 'ctx')
- token_grad: bfloat16 [4, 1024, 4096], P('exp', 'ctx')
The draws below stay inside these ranges and needn't reach their ends.
Inputs may be any that keep to these rules, and one draw needn't show every extreme that they name: `routes`: in the rows of one device no expert is named by more than 24 rows.
All inputs are finite; a program needn't handle non-finite values.
Results may differ from the reference program's by a relative error of at most 0.025.
Values may be sent and summed in bfloat16 or wider, within the bound.
No kernel may reach another device: no remote copies, remote signals or barrier semaphores. Data moves between devices by JAX's collectives and lax.ppermute only.
A program may use at most 192 MiB of HBM per device.

```python
import math
import jax
import jax.numpy as jnp
import numpy as np
from jax import lax

D = 4096
QUERY_HEADS = 32
KEY_VALUE_HEADS = 2
HEAD_SIZE = 128
FF = 1536
TOPK = 2
TOK_DEV = 128
FF_DEV = 768
EXPERTS = 16
CAP = 24
SEQUENCE_COUNT = 4
SEQUENCE_LENGTH = 1024
SPAN = 64
N_CTX = 8
N_EXP = 4


def drawn_parts(key):
    base_offset = jax.random.normal(jax.random.fold_in(key, 101), (SEQUENCE_COUNT, SEQUENCE_LENGTH, KEY_VALUE_HEADS, HEAD_SIZE), jnp.float32)
    return base_offset


def draw_keys(key, part):
    base_offset = drawn_parts(key)
    keyed_scores = jnp.clip(base_offset, -4.5, 4.5)
    return keyed_scores.reshape(SEQUENCE_COUNT, SEQUENCE_LENGTH, KEY_VALUE_HEADS * HEAD_SIZE).astype(jnp.bfloat16)


def draw_queries(key, part):
    key = jax.random.fold_in(key, 8)
    heads_per_group = QUERY_HEADS // KEY_VALUE_HEADS
    mixed_result = jnp.clip(jax.random.normal(key, (SEQUENCE_COUNT, SEQUENCE_LENGTH, KEY_VALUE_HEADS, heads_per_group, HEAD_SIZE), jnp.float32), -4.5, 4.5)
    return mixed_result.reshape(SEQUENCE_COUNT, SEQUENCE_LENGTH, QUERY_HEADS * HEAD_SIZE).astype(jnp.bfloat16)


def shard_levels(stream_key, dims, shards, least, top_value):
    level, own = 1.0, jax.random.fold_in(stream_key, 6)
    for dim, parts in shards:
        heights = jnp.exp(jax.random.uniform(jax.random.fold_in(own, dim), (parts,), jnp.float32, least / len(shards), top_value / len(shards)))
        level = level * jnp.repeat(heights, dims[dim] // parts).reshape([-1 if axis == dim else 1 for axis in range(len(dims))])
    return level


def deal_out(stream_key, own, number, rows, number_of, top, reach, slope):
    sequence = jax.random.permutation(stream_key, number_of)
    crowded, usual = portions_of(number_of, rows * top, reach, slope, True), portions_of(number_of, rows * top, reach, slope, False)
    places = jnp.arange(number_of)

    def named(sizes, turn):
        used = int((sizes > 0).sum())
        fixed = max(1, used // 4)
        moved = fixed + (places - fixed + turn * (used - fixed)) % max(1, number_of - fixed)
        return jnp.zeros((number_of,), jnp.int32).at[sequence[jnp.where(places < fixed, places, moved)]].set(jnp.asarray(sizes, jnp.int32))

    sizes = jnp.where(number % 4 == 0, named(crowded, number // 4), named(usual, number - number // 4 - 1))
    mixed = jax.random.permutation(jax.random.fold_in(own, 3), number_of)
    giver, sink = mixed[0:number_of // 2 * 2:2], mixed[1:number_of // 2 * 2:2]
    slack = jnp.minimum(sizes[giver] - 1, reach - sizes[sink]) // 2
    slack = jnp.where((giver == sequence[0]) | (sink == sequence[0]) | (sizes[sink] == 0), 0, jnp.maximum(slack, 0))
    moved = jax.random.randint(jax.random.fold_in(own, 4), (number_of // 2,), 0, 1 << 20) % (slack + 1)
    sizes = sizes.at[giver].add(-moved).at[sink].add(moved)
    members = jnp.searchsorted(jnp.cumsum(sizes), jnp.arange(rows * top), side="right").astype(jnp.int32)
    grid = members.reshape(top, rows).T
    grid = grid[jax.random.permutation(jax.random.fold_in(own, 1), rows)]
    turn = jax.random.randint(jax.random.fold_in(own, 2), (rows, 1), 0, top)
    return jnp.take_along_axis(grid, (jnp.arange(top)[None, :] + turn) % top, axis=1)


def portions_of(count, total, reach, lean, full):
    loads = [(1 << 20) // math.isqrt(standing ** lean) + 1 for standing in range(1, count + 1)]
    largest = reach if full else min(reach, max(-(-total // count), total * loads[0] // sum(loads)))
    least = 1 if total - largest >= count - 1 else 0
    holding, spare = [largest] + [least] * (count - 1), total - largest - least * (count - 1)
    while spare > 0:
        candidates = [i for i in range(1, count) if holding[i] < largest] or [i for i in range(1, count) if holding[i] < reach]
        whole, budget = sum([loads[i] for i in candidates]), spare
        for i in candidates:
            addition = min(reach - holding[i], max(1, budget * loads[i] // whole), spare)
            holding[i] = holding[i] + addition
            spare = spare - addition
    return np.array(holding)


def gaussian(key, extent, scale, bound, cuts=(), held_as=jnp.bfloat16):
    values = scale * jax.random.normal(key, extent, jnp.float32)
    if cuts:
        values = values * shard_levels(key, extent, cuts, -0.22, 0.18)
    return jnp.clip(values, -bound, bound).astype(held_as)


def setup_inputs(seed: int = 0) -> dict:
    key_list = jax.random.split(jax.random.key(seed), 13)
    queries = draw_queries(jax.random.fold_in(key_list[12], 71), 0)
    keys = draw_keys(jax.random.fold_in(key_list[12], 71), 0)
    values = gaussian(key_list[2], (SEQUENCE_COUNT, SEQUENCE_LENGTH, KEY_VALUE_HEADS * HEAD_SIZE), 2.0, 12.0, ((0, 4), (1, 8)))
    attention_output_grad = gaussian(key_list[3], (SEQUENCE_COUNT, SEQUENCE_LENGTH, QUERY_HEADS * HEAD_SIZE), 3.0, 18.0, ((0, 4), (1, 8)))
    span_order = jax.vmap(lambda own: jax.random.permutation(own, 2 * N_CTX))(jax.random.split(key_list[4], SEQUENCE_COUNT)).reshape((SEQUENCE_COUNT, 2 * N_CTX)).astype(jnp.int32)
    out_grad = gaussian(key_list[5], (SEQUENCE_COUNT, SEQUENCE_LENGTH, D), 1.0, 6.0, ((0, 4), (1, 8)))
    routes_keys = jax.random.split(jax.random.fold_in(key_list[6], 1), SEQUENCE_COUNT * SEQUENCE_LENGTH // TOK_DEV)
    routes_turns = jax.random.permutation(jax.random.fold_in(key_list[6], 3), SEQUENCE_COUNT * SEQUENCE_LENGTH // TOK_DEV)
    routes = jax.vmap(lambda own, number: deal_out(jax.random.fold_in(key_list[6], 2), own, number, TOK_DEV, EXPERTS, TOPK, CAP, 2))(routes_keys, routes_turns).reshape((SEQUENCE_COUNT, SEQUENCE_LENGTH, TOPK))
    combine = jnp.clip(0.1 + 0.9 * jax.random.uniform(key_list[7], (SEQUENCE_COUNT, SEQUENCE_LENGTH, TOPK), jnp.float32) ** shard_levels(key_list[7], (SEQUENCE_COUNT, SEQUENCE_LENGTH, TOPK), ((0, 4), (1, 8)), -0.2, 0.2), 0.1, 1.0)
    w_gate = gaussian(key_list[8], (EXPERTS * 2, D, FF_DEV), D ** -0.5, 0.09375, ((0, 32),))
    w_up = gaussian(key_list[9], (EXPERTS * 2, D, FF_DEV), D ** -0.5, 0.09375, ((0, 32),))
    w_down = gaussian(key_list[10], (EXPERTS * 2, FF_DEV, D), FF ** -0.5, 0.15625, ((0, 32),))
    gate_up_saved = gaussian(key_list[11], (EXPERTS * 2, N_CTX * N_EXP, CAP, 2 * FF_DEV), 1.0, 6.0, ((0, 32),))
    return dict(queries=queries, keys=keys, values=values, attention_output_grad=attention_output_grad, span_order=span_order, out_grad=out_grad, routes=routes, combine=combine, w_gate=w_gate, w_up=w_up, w_down=w_down, gate_up_saved=gate_up_saved)


def attend_sequence(bundle):
    query_sequence, key_sequence, value_sequence, gradient_sequence, span_ids = bundle
    heads_per_group = QUERY_HEADS // KEY_VALUE_HEADS
    score_scale = HEAD_SIZE ** -0.5
    row_ids = jnp.arange(SEQUENCE_LENGTH, dtype=jnp.int32)
    position = span_ids[row_ids // SPAN] * SPAN + row_ids % SPAN
    visible = (position[None, :] <= position[:, None])[None]
    query_full = query_sequence.reshape(SEQUENCE_LENGTH, KEY_VALUE_HEADS, heads_per_group, HEAD_SIZE).astype(jnp.float32)
    gradient_full = gradient_sequence.reshape(SEQUENCE_LENGTH, KEY_VALUE_HEADS, heads_per_group, HEAD_SIZE).astype(jnp.float32)
    key_full = key_sequence.reshape(SEQUENCE_LENGTH, KEY_VALUE_HEADS, HEAD_SIZE).astype(jnp.float32)
    value_full = value_sequence.reshape(SEQUENCE_LENGTH, KEY_VALUE_HEADS, HEAD_SIZE).astype(jnp.float32)
    query_parts, key_sections, value_sections = [], [], []
    for shared_key_head in range(KEY_VALUE_HEADS):
        query_part = query_full[:, shared_key_head]
        grad_part = gradient_full[:, shared_key_head]
        key_part = key_full[:, shared_key_head]
        value_part = value_full[:, shared_key_head]
        scores = jnp.einsum("qgd,kd->gqk", query_part, key_part) * score_scale
        peak = jnp.max(jnp.where(visible, scores, -jnp.inf), axis=-1, keepdims=True)
        summed = jnp.sum(jnp.where(visible, jnp.exp(scores - peak), 0.0), axis=-1, keepdims=True)
        log_total = peak + jnp.log(summed)
        probs = jnp.where(visible, jnp.exp(scores - log_total), 0.0)
        dprobs = jnp.einsum("qgd,kd->gqk", grad_part, value_part)
        delta = jnp.sum(probs * dprobs, axis=-1, keepdims=True)
        dscores = (score_scale * probs * (dprobs - delta)).astype(jnp.bfloat16).astype(jnp.float32)
        probs_low = probs.astype(jnp.bfloat16).astype(jnp.float32)
        query_parts.append(jnp.einsum("gqk,kd->qgd", dscores, key_part))
        key_sections.append(jnp.einsum("gqk,qgd->kd", dscores, query_part))
        value_sections.append(jnp.einsum("gqk,qgd->kd", probs_low, grad_part))
    query_out = jnp.stack(query_parts, axis=1).reshape(SEQUENCE_LENGTH, QUERY_HEADS * HEAD_SIZE).astype(jnp.bfloat16)
    key_result = jnp.stack(key_sections, axis=1).reshape(SEQUENCE_LENGTH, KEY_VALUE_HEADS * HEAD_SIZE).astype(jnp.bfloat16)
    value_result = jnp.stack(value_sections, axis=1).reshape(SEQUENCE_LENGTH, KEY_VALUE_HEADS * HEAD_SIZE).astype(jnp.bfloat16)
    return query_out, key_result, value_result


def reference(queries, keys, values, attention_output_grad, span_order, out_grad, routes, combine, w_gate, w_up, w_down, gate_up_saved):
    query_grad, key_grad, value_grad = lax.map(attend_sequence, (queries, keys, values, attention_output_grad, span_order))
    sources = N_CTX * N_EXP
    pairs = TOK_DEV * TOPK
    slot_grad = (out_grad[:, :, None, :].astype(jnp.float32) * combine[:, :, :, None]).astype(jnp.bfloat16)
    slot_grad = slot_grad.reshape(N_EXP, N_CTX, TOK_DEV, TOPK, D).transpose(1, 0, 2, 3, 4).reshape(sources, pairs, D)
    route_src = routes.reshape(N_EXP, N_CTX, TOK_DEV, TOPK).transpose(1, 0, 2, 3).reshape(sources, pairs)
    named = (route_src[:, :, None] == jnp.arange(EXPERTS, dtype=jnp.int32)[None, None, :]).astype(jnp.int32)
    slot_rank = jnp.sum(named * (jnp.cumsum(named, axis=1) - 1), axis=2).astype(jnp.int32)
    slot_index = route_src * CAP + slot_rank
    source_ids = jnp.arange(sources, dtype=jnp.int32)[:, None]
    buffer = jnp.zeros((sources, EXPERTS * CAP, D), jnp.bfloat16).at[source_ids, slot_index].set(slot_grad)

    def expert_one(expert):
        incoming = lax.dynamic_slice_in_dim(buffer, expert * CAP, CAP, 1).reshape(sources * CAP, D)
        summed = jnp.zeros((sources * CAP, D), jnp.float32)
        for half_index in range(2):
            piece_index = expert * 2 + half_index
            saved_rows = gate_up_saved[piece_index].reshape(sources * CAP, 2 * FF_DEV).astype(jnp.float32)
            gate_pre = saved_rows[:, :FF_DEV]
            up_pre = saved_rows[:, FF_DEV:]
            hidden_grad = jnp.dot(incoming, w_down[piece_index].T, preferred_element_type=jnp.float32)
            sigma = jax.nn.sigmoid(gate_pre)
            gate_grad = (hidden_grad * up_pre * sigma * (1.0 + gate_pre * (1.0 - sigma))).astype(jnp.bfloat16)
            up_grad = (hidden_grad * gate_pre * sigma).astype(jnp.bfloat16)
            summed = summed + jnp.dot(gate_grad, w_gate[piece_index].T, preferred_element_type=jnp.float32)
            summed = summed + jnp.dot(up_grad, w_up[piece_index].T, preferred_element_type=jnp.float32)
        return summed.reshape(sources, CAP, D)

    results = lax.map(expert_one, jnp.arange(EXPERTS, dtype=jnp.int32))
    picked = results[route_src, source_ids, slot_rank]
    token_sum = jnp.sum(picked.reshape(sources, TOK_DEV, TOPK, D), axis=2).astype(jnp.bfloat16)
    token_grad = token_sum.reshape(N_CTX, N_EXP, TOK_DEV, D).transpose(1, 0, 2, 3).reshape(SEQUENCE_COUNT, SEQUENCE_LENGTH, D)
    return query_grad, key_grad, value_grad, token_grad
```

```python
import functools
import math

import jax
import jax.numpy as jnp
from jax import lax
from jax.experimental import pallas as pl
from jax.experimental.pallas import tpu as pltpu
from jax.sharding import PartitionSpec as P

QUERY_HEADS = 32
KEY_VALUE_HEADS = 2
HEAD_SIZE = 128
TOPK = 2
NEG = -1e30
LOG2E = math.log2(math.e)
HEADS_STEP = 8
PARTS = 4
EXTRA = 128
VMEM = 56 * 1024 * 1024


def swap(value, mask):
    count = lax.axis_size("ctx")
    return lax.ppermute(value, "ctx", [(i, i ^ mask) for i in range(count)])


def turn(value, steps=1):
    count = lax.axis_size("exp")
    return lax.ppermute(value, "exp", [(i, (i + steps) % count) for i in range(count)])


def rows_dot(a, b, dims):
    return lax.dot_general(a, b, (dims, ((), ())), preferred_element_type=jnp.float32)


def attention_kernel(
    bias_ref, q_ref, g_ref, k_ref, v_ref, dk_in, dv_in, *refs, after
):
    dq_ref, dk_ref, dv_ref = refs[after:]
    step = pl.program_id(0)
    scale = HEAD_SIZE ** (-0.5)
    heads = q_ref.shape[1] // HEAD_SIZE
    k = k_ref[...]
    v = v_ref[...]
    qs = jnp.concatenate(
        [q_ref[:, h * HEAD_SIZE : (h + 1) * HEAD_SIZE] for h in range(heads)], axis=0
    )
    gs = jnp.concatenate(
        [g_ref[:, h * HEAD_SIZE : (h + 1) * HEAD_SIZE] for h in range(heads)], axis=0
    )
    bias = jnp.concatenate([bias_ref[...]] * heads, axis=1)
    scores = rows_dot(k, qs, ((1,), (1,))) * (scale * LOG2E) + bias
    peak = jnp.max(scores, axis=0, keepdims=True)
    weights = jnp.exp2(scores - peak)
    dprobs = rows_dot(v, gs, ((1,), (1,)))
    total = jnp.sum(weights, axis=0, keepdims=True)
    weighted = jnp.sum(weights * dprobs, axis=0, keepdims=True)
    inverse = 1.0 / total
    delta = weighted * inverse
    probs = weights * inverse
    dscores = (probs * (dprobs - delta) * scale).astype(jnp.bfloat16)
    probs_low = probs.astype(jnp.bfloat16)
    dq = rows_dot(dscores, k, ((0,), (0,)))
    for h in range(heads):
        dq_ref[:, h * HEAD_SIZE : (h + 1) * HEAD_SIZE] = dq[
            h * q_ref.shape[0] : (h + 1) * q_ref.shape[0]
        ].astype(jnp.bfloat16)
    dk = rows_dot(dscores, qs, ((1,), (0,)))
    dv = rows_dot(probs_low, gs, ((1,), (0,)))

    @pl.when(step == 0)
    def _():
        dk_ref[...] = dk_in[...] + dk
        dv_ref[...] = dv_in[...] + dv

    @pl.when(step > 0)
    def _():
        dk_ref[...] += dk
        dv_ref[...] += dv


def attention(part, parts, bias, queries, grads, both, sums, after=()):
    rows = queries.shape[0]
    key_rows = both.shape[0]
    steps = QUERY_HEADS // parts // HEADS_STEP
    group = part * KEY_VALUE_HEADS // parts
    wide = pl.BlockSpec((rows, HEADS_STEP * HEAD_SIZE), lambda i: (0, part * steps + i))
    key_part = pl.BlockSpec((key_rows, HEAD_SIZE), lambda i: (0, group))
    value_part = pl.BlockSpec((key_rows, HEAD_SIZE), lambda i: (0, KEY_VALUE_HEADS + group))
    acc = pl.BlockSpec((key_rows, HEAD_SIZE), lambda i: (0, 0))
    acc_shape = jax.ShapeDtypeStruct((key_rows, HEAD_SIZE), jnp.float32)
    own = pl.BlockSpec((rows, HEADS_STEP * HEAD_SIZE), lambda i: (0, i))
    return pl.pallas_call(
        functools.partial(attention_kernel, after=len(after)),
        grid=(steps,),
        in_specs=[pl.BlockSpec((key_rows, rows), lambda i: (0, 0)), wide, wide]
        + [key_part, value_part, acc, acc]
        + [pl.BlockSpec(memory_space=pl.ANY)] * len(after),
        out_specs=[own, acc, acc],
        out_shape=[
            jax.ShapeDtypeStruct((rows, QUERY_HEADS // parts * HEAD_SIZE), jnp.bfloat16),
            acc_shape,
            acc_shape,
        ],
        compiler_params=pltpu.CompilerParams(vmem_limit_bytes=VMEM),
        name="attention_core",
    )(bias, queries, grads, both, both, *sums, *after)


def pack_kernel(tokens_ref, routes_ref, combine_ref, out_ref):
    rows, width = tokens_ref.shape
    out_ref[:, :width] = tokens_ref[...]
    weights = combine_ref[...]
    high = weights.astype(jnp.bfloat16).astype(jnp.float32)
    names = routes_ref[...].astype(jnp.float32)
    blank = jnp.zeros((EXTRA - 3 * TOPK, rows), jnp.float32)
    flat = jnp.concatenate([names, high, weights - high, blank], axis=0)
    out_ref[:, width:] = flat.T.astype(jnp.bfloat16)


def pack_tokens(tokens, routes, combine):
    rows, width = tokens.shape
    return pl.pallas_call(
        pack_kernel,
        out_shape=jax.ShapeDtypeStruct((rows, width + EXTRA), jnp.bfloat16),
        compiler_params=pltpu.CompilerParams(vmem_limit_bytes=VMEM),
        name="pack_tokens",
    )(tokens, routes.T, combine.T)


def slot_rows(extra_ref, capacity):
    tall = extra_ref[...].astype(jnp.float32)
    flat = tall.T
    tokens = tall.shape[0]
    t_from = lax.broadcasted_iota(jnp.int32, (tokens, tokens), 0)
    t_to = lax.broadcasted_iota(jnp.int32, (tokens, tokens), 1)
    slots = []
    for k in range(TOPK):
        name = flat[k : k + 1]
        rank = 0.0
        for k_from in range(TOPK):
            same = tall[:, k_from : k_from + 1] == name
            earlier = (t_from * TOPK + k_from) < (t_to * TOPK + k)
            rank = rank + jnp.sum(jnp.where(same & earlier, 1.0, 0.0), axis=0, keepdims=True)
        slots.append(name * capacity + rank)
    weights = [flat[TOPK + k : TOPK + k + 1] + flat[2 * TOPK + k : 2 * TOPK + k + 1] for k in range(TOPK)]
    return slots + weights


def slots_kernel(capacity, after, ids_ref, own_x, other_x, own_ref, other_ref, *refs):
    meta_ref, place_ref, factor_ref = refs[-3:]
    outs = refs[after:-3]

    @pl.when(pl.program_id(0) == 0)
    def _():
        places = []
        factor = 0.0
        for rel, extra in enumerate((own_x, other_x)):
            rows = slot_rows(extra, capacity)
            for index, row in enumerate(rows):
                meta_ref[rel, index : index + 1, :] = row
            ids = ids_ref[:, rel : rel + 1]
            first, second = rows[0] == ids, rows[1] == ids
            places.append(jnp.where(first | second, 1.0, 0.0))
            factor = factor + jnp.sum(
                jnp.where(first, rows[2], 0.0) + jnp.where(second, rows[3], 0.0),
                axis=1,
                keepdims=True,
            )
        place_ref[...] = jnp.concatenate(places, axis=1).astype(jnp.bfloat16)
        factor_ref[...] = factor

    tokens = jnp.concatenate([own_ref[...], other_ref[...]], axis=0)
    rows = rows_dot(place_ref[...], tokens, ((1,), (0,))) * factor_ref[...]
    rows = rows.astype(jnp.bfloat16)
    size = outs[0].shape[0]
    for index, out in enumerate(outs):
        out[...] = rows[index * size : (index + 1) * size]


def build_slots(ids, capacity, own, other, pieces, after=(), blocks=2):
    rows = own.shape[0]
    width = own.shape[1] - EXTRA
    size = ids.shape[0] // pieces
    cols = width // blocks
    part = pl.BlockSpec((rows, cols), lambda i: (0, i))
    extra = pl.BlockSpec((rows, EXTRA), lambda i: (0, width // EXTRA))
    out = pl.pallas_call(
        functools.partial(slots_kernel, capacity, len(after)),
        grid=(blocks,),
        in_specs=[pl.BlockSpec(ids.shape, lambda i: (0, 0)), extra, extra, part, part]
        + [pl.BlockSpec(memory_space=pl.ANY)] * len(after),
        out_specs=[pl.BlockSpec((size, cols), lambda i: (0, i))] * pieces
        + [pl.BlockSpec((2, 2 * TOPK, rows), lambda i: (0, 0, 0))],
        out_shape=[jax.ShapeDtypeStruct((size, width), jnp.bfloat16)] * pieces
        + [jax.ShapeDtypeStruct((2, 2 * TOPK, rows), jnp.float32)],
        scratch_shapes=[
            pltpu.VMEM((ids.shape[0], 2 * rows), jnp.bfloat16),
            pltpu.VMEM((ids.shape[0], 1), jnp.float32),
        ],
        compiler_params=pltpu.CompilerParams(vmem_limit_bytes=VMEM),
        name="build_slots",
    )(ids, own, other, own, other, *after)
    return out[:-1], out[-1]


def tokens_kernel(count, adds, ids_ref, meta_ref, *refs):
    pieces, (own_ref, other_ref) = refs[:count], refs[-2:]
    rows = jnp.concatenate([piece[...] for piece in pieces], axis=0)
    for rel, out in ((1, other_ref), (0, own_ref)):
        ids = ids_ref[:, rel : rel + 1]
        place = (meta_ref[rel, 0:1, :] == ids) | (meta_ref[rel, 1:2, :] == ids)
        place = jnp.where(place, 1.0, 0.0).astype(jnp.bfloat16)
        total = rows_dot(place, rows, ((0,), (0,)))
        if adds and rel == 0:
            total = total + refs[count][...].astype(jnp.float32)
        out[...] = total.astype(out.dtype)


def gather_tokens(ids, meta, pieces, received=(), after=(), blocks=2):
    size, width = pieces[0].shape
    tokens = meta.shape[2]
    cols = width // blocks
    part = pl.BlockSpec((size, cols), lambda i: (0, i))
    whole = pl.BlockSpec((tokens, cols), lambda i: (0, i))
    return pl.pallas_call(
        functools.partial(tokens_kernel, len(pieces), len(received)),
        grid=(blocks,),
        in_specs=[
            pl.BlockSpec(ids.shape, lambda i: (0, 0)),
            pl.BlockSpec(meta.shape, lambda i: (0, 0, 0)),
        ]
        + [part] * len(pieces)
        + [whole] * len(received)
        + [pl.BlockSpec(memory_space=pl.ANY)] * len(after),
        out_specs=[whole, whole],
        out_shape=[
            jax.ShapeDtypeStruct((tokens, width), jnp.float32),
            jax.ShapeDtypeStruct((tokens, width), jnp.bfloat16),
        ],
        compiler_params=pltpu.CompilerParams(vmem_limit_bytes=VMEM),
        name="gather_tokens",
    )(ids, meta, *pieces, *received, *after)


def expert_kernel(count, half, after, saved_ref, down_ref, gate_ref, up_ref, *refs):
    pieces, refs = refs[:count], refs[count + after :]
    outs = refs[:count]
    hidden, gate_low, up_low = refs[count:]
    step = pl.program_id(0)
    width = gate_low.shape[1]
    size = outs[0].shape[0]

    @pl.when(step < half)
    def _():
        rows = jnp.concatenate([piece[...] for piece in pieces], axis=0)
        product = rows_dot(rows, down_ref[...], ((1,), (1,)))

        @pl.when(step == 0)
        def _():
            hidden[...] = product

        @pl.when(step > 0)
        def _():
            hidden[...] += product

    @pl.when(step == half)
    def _():
        total = hidden[...]
        gate = saved_ref[:, :width].astype(jnp.float32)
        up = saved_ref[:, width:].astype(jnp.float32)
        sig = 1.0 / (1.0 + jnp.exp(-gate))
        gate_low[...] = (total * up * sig * (1.0 + gate * (1.0 - sig))).astype(jnp.bfloat16)
        up_low[...] = (total * gate * sig).astype(jnp.bfloat16)

    @pl.when(step >= half)
    def _():
        result = rows_dot(gate_low[...], gate_ref[...], ((1,), (1,)))
        result = (result + rows_dot(up_low[...], up_ref[...], ((1,), (1,)))).astype(jnp.bfloat16)
        for index, out in enumerate(outs):
            out[...] = result[index * size : (index + 1) * size]


def expert(saved, w_down, w_gate, w_up, pieces, after=(), half=2):
    size, width = pieces[0].shape
    hidden = w_down.shape[0]
    count = len(pieces)
    cols = width // half
    early = lambda i: (0, jnp.minimum(i, half - 1))
    late = lambda i: (jnp.maximum(i - half, 0), 0)
    rows = size * count
    return pl.pallas_call(
        functools.partial(expert_kernel, count, half, len(after)),
        grid=(2 * half,),
        in_specs=[
            pl.BlockSpec((rows, 2 * hidden), lambda i: (0, 0)),
            pl.BlockSpec((hidden, cols), early),
            pl.BlockSpec((cols, hidden), late),
            pl.BlockSpec((cols, hidden), late),
        ]
        + [pl.BlockSpec((size, cols), early)] * count
        + [pl.BlockSpec(memory_space=pl.ANY)] * len(after),
        out_specs=[pl.BlockSpec((size, cols), lambda i: (0, jnp.maximum(i - half, 0)))] * count,
        out_shape=[jax.ShapeDtypeStruct((size, width), jnp.bfloat16)] * count,
        scratch_shapes=[
            pltpu.VMEM((rows, hidden), jnp.float32),
            pltpu.VMEM((rows, hidden), jnp.bfloat16),
            pltpu.VMEM((rows, hidden), jnp.bfloat16),
        ],
        compiler_params=pltpu.CompilerParams(vmem_limit_bytes=VMEM),
        name="expert_piece",
    )(saved, w_down, w_gate, w_up, *pieces, *after)


def positions(span_ids, row_ids, span):
    slots = jnp.arange(span_ids.shape[0], dtype=jnp.int32)
    found = jnp.sum(
        jnp.where((row_ids // span)[:, None] == slots[None, :], span_ids[None, :], 0), axis=1
    )
    return found * span + row_ids % span


def shards(
    queries,
    keys,
    values,
    attention_output_grad,
    span_order,
    out_grad,
    routes,
    combine,
    w_gate,
    w_up,
    w_down,
    gate_up_saved,
):
    ctx_size = lax.axis_size("ctx")
    exp_size = lax.axis_size("exp")
    ctx_index = lax.axis_index("ctx")
    exp_index = lax.axis_index("exp")
    tokens = queries.shape[1]
    span = tokens // 2
    chips = ctx_size // 2

    capacity = gate_up_saved.shape[2]
    packed = pack_tokens(out_grad[0], routes[0], combine[0])

    both = jnp.concatenate([keys[0], values[0]], axis=1)
    width_kv = keys.shape[2]
    gathered = lax.all_to_all(
        jnp.broadcast_to(both[None], (ctx_size, *both.shape)), "ctx", 0, 0, tiled=True
    )
    gathered = gathered.reshape(ctx_size * tokens, 2 * width_kv)
    row = jnp.arange(ctx_size * tokens, dtype=jnp.int32)
    key_pos = positions(span_order[0], row, span)
    query_pos = positions(
        span_order[0], ctx_index * tokens + jnp.arange(tokens, dtype=jnp.int32), span
    )
    bias = jnp.where(key_pos[:, None] <= query_pos[None, :], 0.0, NEG).astype(jnp.float32)

    padded = -(-capacity // 8) * 8
    m_ids = jnp.arange(chips, dtype=jnp.int32)
    owner = ((ctx_index ^ (2 * m_ids)) * exp_size + exp_index) // 2
    j_ids = jnp.arange(padded, dtype=jnp.int32)
    slot_ids = jnp.where(j_ids < capacity, owner[:, None] * capacity + j_ids, -1)
    rel = jnp.arange(2, dtype=jnp.int32)
    ids = jnp.where(
        rel[None, :, None, None] == rel[None, None, None, :], slot_ids[:, None, :, None], -1
    )
    ids = ids.reshape(chips * 2 * padded, 2).astype(jnp.float32)

    saved = gate_up_saved[0]
    if padded != capacity:
        saved = jnp.pad(saved, ((0, 0), (0, padded - capacity), (0, 0)))
    j_ctx = ctx_index ^ jnp.arange(ctx_size, dtype=jnp.int32)
    s_exp = (exp_index - jnp.arange(exp_size, dtype=jnp.int32)) % exp_size
    picks = (j_ctx[None, :] * exp_size + s_exp[:, None]).reshape(-1)
    saved = jnp.take(saved, picks, axis=0, mode="clip")
    saved = saved.reshape(exp_size, ctx_size * padded, saved.shape[2])

    def across(pieces, gate=()):
        if gate:
            pieces = lax.optimization_barrier((*pieces, *gate))[: len(pieces)]
        return [pieces[0]] + [swap(piece, 2 * m) for m, piece in enumerate(pieces) if m > 0]

    held = [packed]
    other = [swap(packed, 1)]
    last = ()
    slots, sent, rows, results, metas = {}, {}, {}, {}, {}
    attention_parts = []
    zero = jnp.zeros((ctx_size * tokens, HEAD_SIZE), jnp.float32)
    coming = [turn(packed)]

    def arrive(needs=()):
        nonlocal last
        got, *last = lax.optimization_barrier((coming[-1], *last, *needs))
        last = tuple(last[:1])
        held.append(got)
        other.append(swap(got, 1))
        if len(held) < exp_size:
            coming.append(turn(got))

    def build(s, needs=()):
        nonlocal last
        slots[s], metas[s] = build_slots(ids, capacity, held[s], other[s], chips, (*last, *needs))
        last = (slots[s][0],)

    def apply(s, needs=()):
        nonlocal last
        rows[s] = expert(saved[s], w_down[0], w_gate[0], w_up[0], sent[s], (*last, *needs))
        last = (rows[s][0],)

    def gather(s, received=(), needs=()):
        nonlocal last
        own, sibling = gather_tokens(ids, metas[s], results[s], received, (*last, *needs))
        total = own + swap(sibling, 1).astype(jnp.float32)
        total = total.astype(jnp.bfloat16)
        last = (total,)
        return total

    def attend(part, needs=()):
        nonlocal last
        first = part % (PARTS // KEY_VALUE_HEADS) == 0
        sums = (zero, zero) if first else attention_parts[-1][1:]
        done = attention(
            part,
            PARTS,
            bias,
            queries[0],
            attention_output_grad[0],
            gathered,
            sums,
            (*last, *needs),
        )
        last = (done[0],)
        attention_parts.append(done)

    def send(s, gate=()):
        sent[s] = across(slots[s], gate)

    def back(s, gate=()):
        results[s] = across(rows[s], gate)

    build(0)
    send(0)
    attend(0)
    arrive(sent[0][1:])
    attend(1)
    build(1)
    send(1)
    apply(0)
    arrive(sent[1][1:])
    build(2)
    send(2)
    apply(1)
    ring = ()
    for s in range(3, exp_size):
        arrive(sent[s - 1][1:])
        back(s - 2, sent[s - 1][1:])
        if s == 3:
            attend(2)
        build(s)
        if s == 3:
            attend(3)
        send(s, results[s - 2][1:])
        total = gather(s - 2, ring)
        ring = (turn(total),)
        apply(s - 1)
        if s == exp_size - 1:
            back(s - 1, sent[s][1:])
    apply(exp_size - 1, sent[exp_size - 1][1:])
    back(exp_size - 1, results[exp_size - 2][1:])
    ring = (turn(gather(exp_size - 2, ring)),)
    back(0, results[exp_size - 1][1:])
    ring = (turn(gather(exp_size - 1, ring)),)
    token_out = gather(0, ring)[None]

    query_out = jnp.concatenate([done[0] for done in attention_parts], axis=1)
    ends = attention_parts[PARTS // KEY_VALUE_HEADS - 1 :: PARTS // KEY_VALUE_HEADS]
    key_part = jnp.concatenate([done[1] for done in ends], axis=1).astype(jnp.bfloat16)
    value_part = jnp.concatenate([done[2] for done in ends], axis=1).astype(jnp.bfloat16)
    part = jnp.concatenate([key_part, value_part], axis=1)
    part = part.reshape(ctx_size, tokens, 2 * width_kv)
    part = lax.all_to_all(part, "ctx", 0, 0, tiled=True).astype(jnp.float32)
    part = jnp.sum(part, axis=0, keepdims=True).astype(jnp.bfloat16)
    return (query_out[None], part[..., :width_kv], part[..., width_kv:], token_out)


def solution(mesh):
    row = P("exp", "ctx", None)
    piece = P(("ctx", "exp"), None, None)
    in_specs = (row, row, row, row, P("exp", None), row, row, row) + (piece,) * 3 + (
        P(("ctx", "exp"), None, None, None),
    )
    return jax.shard_map(
        shards, mesh=mesh, in_specs=in_specs, out_specs=(row,) * 4, check_vma=False
    )
```

```python
import functools
import math

import jax
import jax.numpy as jnp
from jax import lax
from jax.experimental import pallas as pl
from jax.experimental.pallas import tpu as pltpu
from jax.sharding import PartitionSpec as P

QUERY_HEADS = 32
KEY_VALUE_HEADS = 2
HEAD_SIZE = 128
TOPK = 2
NEG = -1e30
LOG2E = math.log2(math.e)
HEADS_STEP = 8
PARTS = 4
EXTRA = 128
VMEM = 56 * 1024 * 1024


def swap(value, mask):
    count = lax.axis_size("ctx")
    return lax.ppermute(value, "ctx", [(i, i ^ mask) for i in range(count)])


def turn(value, steps=1):
    count = lax.axis_size("exp")
    return lax.ppermute(value, "exp", [(i, (i + steps) % count) for i in range(count)])


def rows_dot(a, b, dims):
    return lax.dot_general(a, b, (dims, ((), ())), preferred_element_type=jnp.float32)


def attention_kernel(
    bias_ref, q_ref, g_ref, k_ref, v_ref, dk_in, dv_in, *refs, after
):
    dq_ref, dk_ref, dv_ref = refs[after:]
    step = pl.program_id(0)
    scale = HEAD_SIZE ** (-0.5)
    heads = q_ref.shape[1] // HEAD_SIZE
    k = k_ref[...]
    v = v_ref[...]
    qs = jnp.concatenate(
        [q_ref[:, h * HEAD_SIZE : (h + 1) * HEAD_SIZE] for h in range(heads)], axis=0
    )
    gs = jnp.concatenate(
        [g_ref[:, h * HEAD_SIZE : (h + 1) * HEAD_SIZE] for h in range(heads)], axis=0
    )
    bias = jnp.concatenate([bias_ref[...]] * heads, axis=1)
    scores = rows_dot(k, qs, ((1,), (1,))) * (scale * LOG2E) + bias
    peak = jnp.max(scores, axis=0, keepdims=True)
    weights = jnp.exp2(scores - peak)
    dprobs = rows_dot(v, gs, ((1,), (1,)))
    total = jnp.sum(weights, axis=0, keepdims=True)
    weighted = jnp.sum(weights * dprobs, axis=0, keepdims=True)
    inverse = 1.0 / total
    delta = weighted * inverse
    probs = weights * inverse
    dscores = (probs * (dprobs - delta) * scale).astype(jnp.bfloat16)
    probs_low = probs.astype(jnp.bfloat16)
    dq = rows_dot(dscores, k, ((0,), (0,)))
    for h in range(heads):
        dq_ref[:, h * HEAD_SIZE : (h + 1) * HEAD_SIZE] = dq[
            h * q_ref.shape[0] : (h + 1) * q_ref.shape[0]
        ].astype(jnp.bfloat16)
    dk = rows_dot(dscores, qs, ((1,), (0,)))
    dv = rows_dot(probs_low, gs, ((1,), (0,)))

    @pl.when(step == 0)
    def _():
        dk_ref[...] = dk_in[...] + dk
        dv_ref[...] = dv_in[...] + dv

    @pl.when(step > 0)
    def _():
        dk_ref[...] += dk
        dv_ref[...] += dv


def attention(part, parts, bias, queries, grads, both, sums, after=()):
    rows = queries.shape[0]
    key_rows = both.shape[0]
    steps = QUERY_HEADS // parts // HEADS_STEP
    group = part * KEY_VALUE_HEADS // parts
    wide = pl.BlockSpec((rows, HEADS_STEP * HEAD_SIZE), lambda i: (0, part * steps + i))
    key_part = pl.BlockSpec((key_rows, HEAD_SIZE), lambda i: (0, group))
    value_part = pl.BlockSpec((key_rows, HEAD_SIZE), lambda i: (0, KEY_VALUE_HEADS + group))
    acc = pl.BlockSpec((key_rows, HEAD_SIZE), lambda i: (0, 0))
    acc_shape = jax.ShapeDtypeStruct((key_rows, HEAD_SIZE), jnp.float32)
    own = pl.BlockSpec((rows, HEADS_STEP * HEAD_SIZE), lambda i: (0, i))
    return pl.pallas_call(
        functools.partial(attention_kernel, after=len(after)),
        grid=(steps,),
        in_specs=[pl.BlockSpec((key_rows, rows), lambda i: (0, 0)), wide, wide]
        + [key_part, value_part, acc, acc]
        + [pl.BlockSpec(memory_space=pl.ANY)] * len(after),
        out_specs=[own, acc, acc],
        out_shape=[
            jax.ShapeDtypeStruct((rows, QUERY_HEADS // parts * HEAD_SIZE), jnp.bfloat16),
            acc_shape,
            acc_shape,
        ],
        compiler_params=pltpu.CompilerParams(vmem_limit_bytes=VMEM),
        name="attention_core",
    )(bias, queries, grads, both, both, *sums, *after)


def pack_kernel(tokens_ref, routes_ref, combine_ref, out_ref):
    rows, width = tokens_ref.shape
    out_ref[:, :width] = tokens_ref[...]
    weights = combine_ref[...]
    high = weights.astype(jnp.bfloat16).astype(jnp.float32)
    names = routes_ref[...].astype(jnp.float32)
    blank = jnp.zeros((EXTRA - 3 * TOPK, rows), jnp.float32)
    flat = jnp.concatenate([names, high, weights - high, blank], axis=0)
    out_ref[:, width:] = flat.T.astype(jnp.bfloat16)


def pack_tokens(tokens, routes, combine):
    rows, width = tokens.shape
    return pl.pallas_call(
        pack_kernel,
        out_shape=jax.ShapeDtypeStruct((rows, width + EXTRA), jnp.bfloat16),
        compiler_params=pltpu.CompilerParams(vmem_limit_bytes=VMEM),
        name="pack_tokens",
    )(tokens, routes.T, combine.T)


def slot_rows(extra_ref, capacity):
    tall = extra_ref[...].astype(jnp.float32)
    flat = tall.T
    tokens = tall.shape[0]
    t_from = lax.broadcasted_iota(jnp.int32, (tokens, tokens), 0)
    t_to = lax.broadcasted_iota(jnp.int32, (tokens, tokens), 1)
    slots = []
    for k in range(TOPK):
        name = flat[k : k + 1]
        rank = 0.0
        for k_from in range(TOPK):
            same = tall[:, k_from : k_from + 1] == name
            earlier = (t_from * TOPK + k_from) < (t_to * TOPK + k)
            rank = rank + jnp.sum(jnp.where(same & earlier, 1.0, 0.0), axis=0, keepdims=True)
        slots.append(name * capacity + rank)
    weights = [flat[TOPK + k : TOPK + k + 1] + flat[2 * TOPK + k : 2 * TOPK + k + 1] for k in range(TOPK)]
    return slots + weights


def slots_kernel(capacity, after, ids_ref, own_x, other_x, own_ref, other_ref, *refs):
    meta_ref, place_ref, factor_ref = refs[-3:]
    outs = refs[after:-3]

    @pl.when(pl.program_id(0) == 0)
    def _():
        places = []
        factor = 0.0
        for rel, extra in enumerate((own_x, other_x)):
            rows = slot_rows(extra, capacity)
            for index, row in enumerate(rows):
                meta_ref[rel, index : index + 1, :] = row
            ids = ids_ref[:, rel : rel + 1]
            first, second = rows[0] == ids, rows[1] == ids
            places.append(jnp.where(first | second, 1.0, 0.0))
            factor = factor + jnp.sum(
                jnp.where(first, rows[2], 0.0) + jnp.where(second, rows[3], 0.0),
                axis=1,
                keepdims=True,
            )
        place_ref[...] = jnp.concatenate(places, axis=1).astype(jnp.bfloat16)
        factor_ref[...] = factor

    tokens = jnp.concatenate([own_ref[...], other_ref[...]], axis=0)
    rows = rows_dot(place_ref[...], tokens, ((1,), (0,))) * factor_ref[...]
    rows = rows.astype(jnp.bfloat16)
    size = outs[0].shape[0]
    for index, out in enumerate(outs):
        out[...] = rows[index * size : (index + 1) * size]


def build_slots(ids, capacity, own, other, pieces, after=(), blocks=2):
    rows = own.shape[0]
    width = own.shape[1] - EXTRA
    size = ids.shape[0] // pieces
    cols = width // blocks
    part = pl.BlockSpec((rows, cols), lambda i: (0, i))
    extra = pl.BlockSpec((rows, EXTRA), lambda i: (0, width // EXTRA))
    out = pl.pallas_call(
        functools.partial(slots_kernel, capacity, len(after)),
        grid=(blocks,),
        in_specs=[pl.BlockSpec(ids.shape, lambda i: (0, 0)), extra, extra, part, part]
        + [pl.BlockSpec(memory_space=pl.ANY)] * len(after),
        out_specs=[pl.BlockSpec((size, cols), lambda i: (0, i))] * pieces
        + [pl.BlockSpec((2, 2 * TOPK, rows), lambda i: (0, 0, 0))],
        out_shape=[jax.ShapeDtypeStruct((size, width), jnp.bfloat16)] * pieces
        + [jax.ShapeDtypeStruct((2, 2 * TOPK, rows), jnp.float32)],
        scratch_shapes=[
            pltpu.VMEM((ids.shape[0], 2 * rows), jnp.bfloat16),
            pltpu.VMEM((ids.shape[0], 1), jnp.float32),
        ],
        compiler_params=pltpu.CompilerParams(vmem_limit_bytes=VMEM),
        name="build_slots",
    )(ids, own, other, own, other, *after)
    return out[:-1], out[-1]


def tokens_kernel(count, adds, ids_ref, meta_ref, *refs):
    pieces, out = refs[:count], refs[-1]
    rows = jnp.concatenate([piece[...] for piece in pieces], axis=0)
    ids = ids_ref[...]
    place = (meta_ref[0, 0:1, :] == ids) | (meta_ref[0, 1:2, :] == ids)
    place = jnp.where(place, 1.0, 0.0).astype(jnp.bfloat16)
    total = rows_dot(place, rows, ((0,), (0,)))
    if adds:
        total = total + refs[count][...].astype(jnp.float32)
    out[...] = total.astype(out.dtype)


def gather_tokens(ids, meta, pieces, received=(), after=(), blocks=2):
    size, width = pieces[0].shape
    tokens = meta.shape[2]
    cols = width // blocks
    part = pl.BlockSpec((size, cols), lambda i: (0, i))
    whole = pl.BlockSpec((tokens, cols), lambda i: (0, i))
    return pl.pallas_call(
        functools.partial(tokens_kernel, len(pieces), len(received)),
        grid=(blocks,),
        in_specs=[
            pl.BlockSpec(ids.shape, lambda i: (0, 0)),
            pl.BlockSpec(meta.shape, lambda i: (0, 0, 0)),
        ]
        + [part] * len(pieces)
        + [whole] * len(received)
        + [pl.BlockSpec(memory_space=pl.ANY)] * len(after),
        out_specs=whole,
        out_shape=jax.ShapeDtypeStruct((tokens, width), jnp.bfloat16),
        compiler_params=pltpu.CompilerParams(vmem_limit_bytes=VMEM),
        name="gather_tokens",
    )(ids, meta, *pieces, *received, *after)


def expert_kernel(count, half, after, place_ref, saved_ref, down_ref, gate_ref, up_ref, *refs):
    pieces, refs = refs[:count], refs[count + after :]
    out_ref, hidden, gate_low, up_low = refs
    step = pl.program_id(0)
    width = gate_low.shape[1]
    targets, size = out_ref.shape[:2]

    @pl.when(step < half)
    def _():
        rows = jnp.concatenate([piece[...] for piece in pieces], axis=0)
        product = rows_dot(rows, down_ref[...], ((1,), (1,)))

        @pl.when(step == 0)
        def _():
            hidden[...] = product

        @pl.when(step > 0)
        def _():
            hidden[...] += product

    @pl.when(step == half)
    def _():
        total = hidden[...]
        gate = saved_ref[:, :width].astype(jnp.float32)
        up = saved_ref[:, width:].astype(jnp.float32)
        sig = 1.0 / (1.0 + jnp.exp(-gate))
        gate_low[...] = (total * up * sig * (1.0 + gate * (1.0 - sig))).astype(jnp.bfloat16)
        up_low[...] = (total * gate * sig).astype(jnp.bfloat16)

    @pl.when(step >= half)
    def _():
        result = rows_dot(gate_low[...], gate_ref[...], ((1,), (1,)))
        result = result + rows_dot(up_low[...], up_ref[...], ((1,), (1,)))
        for index in range(targets):
            block = result[index * size : (index + 1) * size]
            out_ref[place_ref[0] ^ index] = block.astype(jnp.bfloat16)


def expert(place, targets, saved, w_down, w_gate, w_up, pieces, after=(), half=2):
    size, width = pieces[0].shape
    hidden = w_down.shape[0]
    count = len(pieces)
    cols = width // half
    early = lambda i: (0, jnp.minimum(i, half - 1))
    late = lambda i: (jnp.maximum(i - half, 0), 0)
    rows = size * count
    return pl.pallas_call(
        functools.partial(expert_kernel, count, half, len(after)),
        grid=(2 * half,),
        in_specs=[
            pl.BlockSpec(memory_space=pltpu.SMEM),
            pl.BlockSpec((rows, 2 * hidden), lambda i: (0, 0)),
            pl.BlockSpec((hidden, cols), early),
            pl.BlockSpec((cols, hidden), late),
            pl.BlockSpec((cols, hidden), late),
        ]
        + [pl.BlockSpec((size, cols), early)] * count
        + [pl.BlockSpec(memory_space=pl.ANY)] * len(after),
        out_specs=pl.BlockSpec(
            (targets, rows // targets, cols), lambda i: (0, 0, jnp.maximum(i - half, 0))
        ),
        out_shape=jax.ShapeDtypeStruct((targets, rows // targets, width), jnp.bfloat16),
        scratch_shapes=[
            pltpu.VMEM((rows, hidden), jnp.float32),
            pltpu.VMEM((rows, hidden), jnp.bfloat16),
            pltpu.VMEM((rows, hidden), jnp.bfloat16),
        ],
        compiler_params=pltpu.CompilerParams(vmem_limit_bytes=VMEM),
        name="expert_piece",
    )(place, saved, w_down, w_gate, w_up, *pieces, *after)


def positions(span_ids, row_ids, span):
    slots = jnp.arange(span_ids.shape[0], dtype=jnp.int32)
    found = jnp.sum(
        jnp.where((row_ids // span)[:, None] == slots[None, :], span_ids[None, :], 0), axis=1
    )
    return found * span + row_ids % span


def shards(
    queries,
    keys,
    values,
    attention_output_grad,
    span_order,
    out_grad,
    routes,
    combine,
    w_gate,
    w_up,
    w_down,
    gate_up_saved,
):
    ctx_size = lax.axis_size("ctx")
    exp_size = lax.axis_size("exp")
    ctx_index = lax.axis_index("ctx")
    exp_index = lax.axis_index("exp")
    tokens = queries.shape[1]
    span = tokens // 2
    chips = ctx_size // 2

    capacity = gate_up_saved.shape[2]
    packed = pack_tokens(out_grad[0], routes[0], combine[0])

    both = jnp.concatenate([keys[0], values[0]], axis=1)
    width_kv = keys.shape[2]
    gathered = lax.all_to_all(
        jnp.broadcast_to(both[None], (ctx_size, *both.shape)), "ctx", 0, 0, tiled=True
    )
    gathered = gathered.reshape(ctx_size * tokens, 2 * width_kv)
    row = jnp.arange(ctx_size * tokens, dtype=jnp.int32)
    key_pos = positions(span_order[0], row, span)
    query_pos = positions(
        span_order[0], ctx_index * tokens + jnp.arange(tokens, dtype=jnp.int32), span
    )
    bias = jnp.where(key_pos[:, None] <= query_pos[None, :], 0.0, NEG).astype(jnp.float32)

    padded = -(-capacity // 8) * 8
    m_ids = jnp.arange(chips, dtype=jnp.int32)
    owner = ((ctx_index ^ (2 * m_ids)) * exp_size + exp_index) // 2
    j_ids = jnp.arange(padded, dtype=jnp.int32)
    slot_ids = jnp.where(j_ids < capacity, owner[:, None] * capacity + j_ids, -1)
    rel = jnp.arange(2, dtype=jnp.int32)
    ids = jnp.where(
        rel[None, :, None, None] == rel[None, None, None, :], slot_ids[:, None, :, None], -1
    )
    ids = ids.reshape(chips * 2 * padded, 2).astype(jnp.float32)

    back_owner = (jnp.arange(ctx_size, dtype=jnp.int32) * exp_size + exp_index) // 2
    back_ids = jnp.where(j_ids < capacity, back_owner[:, None] * capacity + j_ids, -1)
    back_ids = back_ids.reshape(ctx_size * padded, 1).astype(jnp.float32)

    saved = gate_up_saved[0]
    if padded != capacity:
        saved = jnp.pad(saved, ((0, 0), (0, padded - capacity), (0, 0)))
    j_ctx = ctx_index ^ jnp.arange(ctx_size, dtype=jnp.int32)
    s_exp = (exp_index - jnp.arange(exp_size, dtype=jnp.int32)) % exp_size
    picks = (j_ctx[None, :] * exp_size + s_exp[:, None]).reshape(-1)
    saved = jnp.take(saved, picks, axis=0, mode="clip")
    saved = saved.reshape(exp_size, ctx_size * padded, saved.shape[2])

    def across(pieces):
        return [pieces[0]] + [swap(piece, 2 * m) for m, piece in enumerate(pieces) if m > 0]

    held = [packed]
    other = [swap(packed, 1)]
    last = ()
    slots, sent, rows, results, metas = {}, {}, {}, {}, {}
    attention_parts = []
    zero = jnp.zeros((ctx_size * tokens, HEAD_SIZE), jnp.float32)
    coming = [turn(packed)]

    def arrive(needs=()):
        nonlocal last
        got, *last = lax.optimization_barrier((coming[-1], *last, *needs))
        last = tuple(last[:1])
        held.append(got)
        other.append(swap(got, 1))
        if len(held) < exp_size:
            coming.append(turn(got))

    def build(s, needs=()):
        nonlocal last
        slots[s], metas[s] = build_slots(ids, capacity, held[s], other[s], chips, (*last, *needs))
        last = (slots[s][0],)

    place = ctx_index.astype(jnp.int32)[None]

    def apply(s, needs=()):
        nonlocal last
        rows[s] = expert(
            place, ctx_size, saved[s], w_down[0], w_gate[0], w_up[0], sent[s], (*last, *needs)
        )
        last = (rows[s],)

    def back(s, gate=()):
        leaving = lax.optimization_barrier((rows[s], *gate))[0] if gate else rows[s]
        came = lax.all_to_all(leaving, "ctx", 0, 0, tiled=True)
        results[s] = [came.reshape(ctx_size * padded, came.shape[2])]

    def gather(s, received=(), needs=()):
        nonlocal last
        total = gather_tokens(back_ids, metas[s], results[s], received, (*last, *needs))
        last = (total,)
        return total

    def attend(part, needs=()):
        nonlocal last
        first = part % (PARTS // KEY_VALUE_HEADS) == 0
        sums = (zero, zero) if first else attention_parts[-1][1:]
        done = attention(
            part,
            PARTS,
            bias,
            queries[0],
            attention_output_grad[0],
            gathered,
            sums,
            (*last, *needs),
        )
        last = (done[0],)
        attention_parts.append(done)

    def send(s, gate=()):
        pieces = list(slots[s])
        if gate:
            pieces = list(lax.optimization_barrier((*pieces, *gate))[: len(pieces)])
        sent[s] = across(pieces)

    build(0)
    near = [m for m in range(1, chips) if m & (m - 1) == 0]
    far = [m for m in range(1, chips) if m & (m - 1)]
    first = {m: swap(slots[0][m], 2 * m) for m in near}
    attend(0)
    arrive([first[m] for m in near])
    late = lax.optimization_barrier((held[1], *[slots[0][m] for m in far]))[1:]
    first.update({m: swap(piece, 2 * m) for m, piece in zip(far, late)})
    sent[0] = [slots[0][0]] + [first[m] for m in range(1, chips)]
    build(1)
    send(1)
    attend(1)
    attend(2)
    arrive([*sent[1][1:], *(first[m] for m in far)])
    build(2)
    send(2)
    apply(1)
    ring = ()
    for s in range(3, exp_size):
        arrive(sent[s - 1][1:])
        back(s - 2, last)
        build(s)
        send(s)
        apply(s - 1)
        ring = (turn(gather(s - 2, ring, sent[s][1:])),)
    back(exp_size - 2, last)
    apply(exp_size - 1)
    apply(0)
    ring = (turn(gather(exp_size - 2, ring)),)
    back(exp_size - 1, last)
    attend(3)
    ring = (turn(gather(exp_size - 1, ring)),)
    after_rings = last
    back(0, last)
    token_out = gather(0, ring)[None]

    query_out = jnp.concatenate([done[0] for done in attention_parts], axis=1)
    ends = attention_parts[PARTS // KEY_VALUE_HEADS - 1 :: PARTS // KEY_VALUE_HEADS]
    key_part = jnp.concatenate([done[1] for done in ends], axis=1).astype(jnp.bfloat16)
    value_part = jnp.concatenate([done[2] for done in ends], axis=1).astype(jnp.bfloat16)
    part = jnp.concatenate([key_part, value_part], axis=1)
    part = lax.optimization_barrier((part, *after_rings))[0]
    part = part.reshape(ctx_size, tokens, 2 * width_kv)
    mask = 1
    while mask < ctx_size:
        pair = part.reshape(part.shape[0] // 2, 2, tokens, 2 * width_kv)
        upper = (ctx_index // mask) % 2 == 1
        mine = jnp.where(upper, pair[:, 1], pair[:, 0]).astype(jnp.float32)
        yours = jnp.where(upper, pair[:, 0], pair[:, 1]).astype(jnp.bfloat16)
        part = mine + swap(yours, mask).astype(jnp.float32)
        mask *= 2
    part = part.astype(jnp.bfloat16)
    return (query_out[None], part[..., :width_kv], part[..., width_kv:], token_out)


def solution(mesh):
    row = P("exp", "ctx", None)
    piece = P(("ctx", "exp"), None, None)
    in_specs = (row, row, row, row, P("exp", None), row, row, row) + (piece,) * 3 + (
        P(("ctx", "exp"), None, None, None),
    )
    return jax.shard_map(
        shards, mesh=mesh, in_specs=in_specs, out_specs=(row,) * 4, check_vma=False
    )
```
